256 devices in a mesh: row: 16 (over y, x), col: 16 (over z, core).
Axes of the slice: x: 4, y: 4, z: 8, core: 2. Of those that a mesh axis runs over, the one named last changes fastest.
Arguments:
- activations: bfloat16 [512, 8192], P('col', 'row'), may hold values from -6 to 6
- cotangent: bfloat16 [512, 8192], P('row', 'col'), may hold values from -6 to 6
- gate_base: bfloat16 [8192, 29568], P('row', 'col'), may hold values from -0.0625 to 0.0625
- up_base: bfloat16 [8192, 29568], P('row', 'col'), may hold values from -0.0625 to 0.0625
- down_base: bfloat16 [29568, 8192], P('row', 'col'), may hold values from -0.03125 to 0.03125
- gate_left: float32 [32, 8192], P(None, 'row'), may hold values from -1.75 to 1.75
- gate_right: float32 [32, 29568], P(None, 'col'), may hold values from -1.75 to 1.75
- up_left: float32 [32, 8192], P(None, 'row'), may hold values from -1.75 to 1.75
- up_right: float32 [32, 29568], P(None, 'col'), may hold values from -1.75 to 1.75
- down_left: float32 [32, 29568], P(None, 'row'), may hold values from -1.75 to 1.75
- down_right: float32 [32, 8192], P(None, 'col'), may hold values from -1.75 to 1.75
Outputs:
- grad_input: bfloat16 [512, 8192], P('col', 'row')
- grad_gate_left: float32 [32, 8192], P(None, 'row')
- grad_gate_right: float32 [32, 29568], P(None, 'col')
- grad_up_left: float32 [32, 8192], P(None, 'row')
- grad_up_right: float32 [32, 29568], P(None, 'col')
- grad_down_left: float32 [32, 29568], P(None, 'row')
- grad_down_right: float32 [32, 8192], P(None, 'col')
The draws below stay inside these ranges and needn't reach their ends.
All inputs are finite; a program needn't handle non-finite values.
Results may differ from the reference program's by a relative error of at most 0.0072.
Values may be sent and summed in bfloat16 or wider, within the bound.
No kernel may reach another device: no remote copies, remote signals or barrier semaphores. Data moves between devices by JAX's collectives and lax.ppermute only.
A program may use at most 128 MiB of HBM per device.

```python
import jax
import jax.numpy as jnp
from jax import lax

D = 8192
FF = 29568
RANK = 32
TOKENS = 512
N_COL = 16


def block_levels(own_key, dims, pieces, low, largest):
    gain, own = 1.0, jax.random.fold_in(own_key, 6)
    for axis_at, blocks in pieces:
        steps = jnp.exp(jax.random.uniform(jax.random.fold_in(own, axis_at), (blocks,), jnp.float32, low / len(pieces), largest / len(pieces)))
        gain = gain * jnp.repeat(steps, dims[axis_at] // blocks).reshape([-1 if axis == axis_at else 1 for axis in range(len(dims))])
    return gain


def bell_draw(rng, dims, deviation, bound, split=(), kind=jnp.bfloat16):
    drawn = jax.random.normal(rng, dims, jnp.float32) * deviation
    if len(split) > 0:
        drawn = block_levels(rng, dims, split, -0.22, 0.18) * drawn
    return jnp.clip(drawn, min=-bound, max=bound).astype(kind)


def setup_inputs(seed: int = 0) -> dict:
    splits = jax.random.split(jax.random.key(seed), 12)
    return {
        "activations": bell_draw(splits[0], (TOKENS, D), 1.0, 6.0, ((0, 16), (1, 16))),
        "cotangent": bell_draw(splits[1], (TOKENS, D), 1.0, 6.0, ((0, 16), (1, 16))),
        "gate_base": bell_draw(splits[2], (D, FF), D ** -0.5, 0.0625, ((0, 16), (1, 16))),
        "up_base": bell_draw(splits[3], (D, FF), D ** -0.5, 0.0625, ((0, 16), (1, 16))),
        "down_base": bell_draw(splits[4], (FF, D), FF ** -0.5, 0.03125, ((0, 16), (1, 16))),
        "gate_left": bell_draw(splits[5], (RANK, D), 0.3, 1.75, ((1, 16),), jnp.float32),
        "gate_right": bell_draw(splits[6], (RANK, FF), 0.3, 1.75, ((1, 16),), jnp.float32),
        "up_left": bell_draw(splits[7], (RANK, D), 0.3, 1.75, ((1, 16),), jnp.float32),
        "up_right": bell_draw(splits[8], (RANK, FF), 0.3, 1.75, ((1, 16),), jnp.float32),
        "down_left": bell_draw(splits[9], (RANK, FF), 0.3, 1.75, ((1, 16),), jnp.float32),
        "down_right": bell_draw(splits[10], (RANK, D), 0.3, 1.75, ((1, 16),), jnp.float32),
    }


HIGHEST_PREC = lax.Precision.HIGHEST


def effective(base, left, right):
    lowrank = jnp.dot(left.T, right, precision=HIGHEST_PREC, preferred_element_type=jnp.float32)
    return (base.astype(jnp.float32) * (1.0 + lowrank)).astype(jnp.bfloat16)


def swish_parts(gate_z, up_z, grad_h):
    squash = jax.nn.sigmoid(gate_z)
    swished = gate_z * squash
    hidden = (swished * up_z).astype(jnp.bfloat16)
    d_up = (grad_h * swished).astype(jnp.bfloat16)
    d_gate = (grad_h * up_z * squash * (1.0 + gate_z * (1.0 - squash))).astype(jnp.bfloat16)
    return hidden, d_gate, d_up


def reference(activations, cotangent, gate_base, up_base, down_base, gate_left, gate_right, up_left, up_right, down_left, down_right):
    block_width = FF // N_COL
    block_count = FF // block_width

    def one_block(carry, block_index):
        dx_acc, gl_acc, ul_acc, dr_acc = carry
        offset = (block_index * block_width).astype(jnp.int32)
        gate_tile = lax.dynamic_slice_in_dim(gate_base, offset, block_width, 1)
        up_tile = lax.dynamic_slice_in_dim(up_base, offset, block_width, 1)
        down_tile = lax.dynamic_slice_in_dim(down_base, offset, block_width, 0)
        gate_rt = lax.dynamic_slice_in_dim(gate_right, offset, block_width, 1)
        up_rt = lax.dynamic_slice_in_dim(up_right, offset, block_width, 1)
        down_lt = lax.dynamic_slice_in_dim(down_left, offset, block_width, 1)
        gate_eff = effective(gate_tile, gate_left, gate_rt)
        up_eff = effective(up_tile, up_left, up_rt)
        down_eff = effective(down_tile, down_lt, down_right)
        gate_z = jnp.dot(activations, gate_eff, preferred_element_type=jnp.float32)
        up_z = jnp.dot(activations, up_eff, preferred_element_type=jnp.float32)
        grad_h = jnp.dot(cotangent, down_eff.T, preferred_element_type=jnp.float32)
        hidden, d_gate, d_up = swish_parts(gate_z, up_z, grad_h)
        full_down = jnp.dot(hidden.T, cotangent, preferred_element_type=jnp.float32)
        full_gate = jnp.dot(activations.T, d_gate, preferred_element_type=jnp.float32)
        full_up = jnp.dot(activations.T, d_up, preferred_element_type=jnp.float32)
        dx_acc = dx_acc + jnp.dot(d_gate, gate_eff.T, preferred_element_type=jnp.float32)
        dx_acc = dx_acc + jnp.dot(d_up, up_eff.T, preferred_element_type=jnp.float32)
        masked_gate = full_gate * gate_tile.astype(jnp.float32)
        masked_up = full_up * up_tile.astype(jnp.float32)
        masked_down = full_down * down_tile.astype(jnp.float32)
        gl_acc = gl_acc + jnp.dot(gate_rt, masked_gate.T, precision=HIGHEST_PREC, preferred_element_type=jnp.float32)
        ul_acc = ul_acc + jnp.dot(up_rt, masked_up.T, precision=HIGHEST_PREC, preferred_element_type=jnp.float32)
        dr_acc = dr_acc + jnp.dot(down_lt, masked_down, precision=HIGHEST_PREC, preferred_element_type=jnp.float32)
        gr_out = jnp.dot(gate_left, masked_gate, precision=HIGHEST_PREC, preferred_element_type=jnp.float32)
        ur_out = jnp.dot(up_left, masked_up, precision=HIGHEST_PREC, preferred_element_type=jnp.float32)
        dl_out = jnp.dot(down_right, masked_down.T, precision=HIGHEST_PREC, preferred_element_type=jnp.float32)
        return (dx_acc, gl_acc, ul_acc, dr_acc), (gr_out, ur_out, dl_out)

    start_carry = (jnp.zeros((TOKENS, D), jnp.float32), jnp.zeros((RANK, D), jnp.float32),
                   jnp.zeros((RANK, D), jnp.float32), jnp.zeros((RANK, D), jnp.float32))
    carry, stacked = lax.scan(one_block, start_carry, jnp.arange(block_count, dtype=jnp.int32))
    dx_acc, gl_acc, ul_acc, dr_acc = carry

    def unstack(parts):
        return parts.transpose(1, 0, 2).reshape(RANK, FF)

    return (dx_acc.astype(jnp.bfloat16), gl_acc, unstack(stacked[0]), ul_acc, unstack(stacked[1]),
            unstack(stacked[2]), dr_acc)
```

```python
import jax
import jax.numpy as jnp
from jax import lax
from jax.experimental import pallas as pl
from jax.experimental.pallas import tpu as pltpu
from jax.sharding import Mesh, PartitionSpec as P

F32 = jnp.float32
BF16 = jnp.bfloat16
NY, NX, NZ, NC = 4, 4, 8, 2
SIZES = {"y": NY, "x": NX, "z": NZ, "core": NC}
ROW = ("y", "x")
COL = ("z", "core")
TILE = 256
VMEM_LIMIT = 48 * 1024 * 1024


def tiles(width):
    return [(at, min(at + TILE, width)) for at in range(0, width, TILE)]


def vmem():
    return pl.BlockSpec(memory_space=pltpu.VMEM)


def smem():
    return pl.BlockSpec(memory_space=pltpu.SMEM)


def kernel_call(body, ids, args, outs, scratch=(), flops=0):
    size = sum(a.size * a.dtype.itemsize for a in args)
    return pl.pallas_call(
        body,
        out_shape=[jax.ShapeDtypeStruct(s, d) for s, d in outs],
        in_specs=[smem()] + [vmem()] * len(args),
        out_specs=[vmem()] * len(outs),
        scratch_shapes=list(scratch),
        compiler_params=pltpu.CompilerParams(vmem_limit_bytes=VMEM_LIMIT),
        cost_estimate=pl.CostEstimate(flops=flops, bytes_accessed=size, transcendentals=0),
    )(ids, *args)


def shift(v, axis, step):
    n = SIZES[axis]
    return lax.ppermute(v, axis, [(i, (i + step) % n) for i in range(n)])


def transpose_grid(v):
    perm = [(a * 16 + b, b * 16 + a) for a in range(16) for b in range(16)]
    return lax.ppermute(v, ("y", "x", "z", "core"), perm)


def add_all(*vs):
    total = vs[0].astype(F32)
    for v in vs[1:]:
        total = total + v.astype(F32)
    return total


def halves(v):
    high = lax.reduce_precision(v, 8, 7)
    return high.astype(BF16), (v - high).astype(BF16)


def effective(base, left, right):
    lh, ll = halves(left)
    rh, rl = halves(right)
    lowrank = lax.dot_general(
        jnp.concatenate([lh, ll, lh], axis=0),
        jnp.concatenate([rh, rh, rl], axis=0),
        (((0,), (0,)), ((), ())),
        preferred_element_type=F32,
    )
    return (base.astype(F32) * (1.0 + lowrank)).astype(BF16)


def swish_parts(gate_z, up_z, grad_h):
    squash = jax.nn.sigmoid(gate_z)
    swished = gate_z * squash
    hidden = (swished * up_z).astype(BF16)
    d_up = (grad_h * swished).astype(BF16)
    d_gate = (grad_h * up_z * squash * (1.0 + gate_z * (1.0 - squash))).astype(BF16)
    return hidden, d_gate, d_up


def nt(a, b):
    return lax.dot_general(a, b, (((1,), (1,)), ((), ())), preferred_element_type=F32)


def tn(a, b):
    return lax.dot_general(a, b, (((0,), (0,)), ((), ())), preferred_element_type=F32)


def nn(a, b):
    return jnp.dot(a, b, preferred_element_type=F32)


def regroup(v):
    return v.reshape(4, 4, 32, v.shape[-1]).swapaxes(0, 1).reshape(v.shape)


def gate_body(ids, act, eff, c0, c1, c2, c3, rel):
    y, x = ids[0], ids[1]
    for dx in range(4):
        for dy in range(4):
            block = lax.rem(y + dy, 4) * 4 + lax.rem(x + dx, 4)
            at = (dx * 4 + dy) * 32
            rel[at : at + 32, :] = act[block]
    a = rel[...]
    for lo, hi in tiles(eff.shape[1]):
        r = nn(a, eff[:, lo:hi])
        for k, out in enumerate((c0, c1, c2, c3)):
            out[:, lo:hi] = r[k * 128 : (k + 1) * 128].astype(out.dtype)


def up_body(ids, rel, eff, c0, c1, c2, c3):
    a = regroup(rel[...])
    for lo, hi in tiles(eff.shape[1]):
        r = nn(a, eff[:, lo:hi])
        for k, out in enumerate((c0, c1, c2, c3)):
            out[:, lo:hi] = r[k * 128 : (k + 1) * 128].astype(out.dtype)


def hid_body(ids, cot, eff, own, other, rel):
    core = ids[3]
    for k in range(2):
        for z in range(8):
            block = z * 2 + lax.rem(core + k, 2)
            at = (k * 8 + z) * 32
            rel[at : at + 32, :] = cot[block]
    a = rel[...]
    for lo, hi in tiles(eff.shape[0]):
        r = nt(a, eff[lo:hi, :])
        own[:, lo:hi] = r[:256].astype(own.dtype)
        other[:, lo:hi] = r[256:].astype(other.dtype)


def factor_sums(m, left, right):
    lp = nt(right, m)
    rp = nn(left, m)
    return lp[:32] + lp[32:], rp[:32] + rp[32:]


def gate_grad_body(ids, g0, g1, g2, g3, rel, base, eff, left, right, gi, lpart, rpart):
    width = base.shape[1]
    a = rel[...]
    for n, (lo, hi) in enumerate(tiles(width)):
        g = jnp.concatenate([r[:, lo:hi] for r in (g0, g1, g2, g3)], axis=0)
        term = nt(g, eff[:, lo:hi])
        m = (tn(a, g) * base[:, lo:hi].astype(F32)).astype(BF16)
        lp, rp = factor_sums(m, left[...], right[:, lo:hi])
        rpart[:, lo:hi] = rp
        if n == 0:
            gi[...] = term
            lpart[...] = lp
        else:
            gi[...] += term
            lpart[...] += lp


def up_grad_body(ids, g0, g1, g2, g3, rel, base, eff, left, right, gi, own, other, lpart, rpart, acc):
    width = base.shape[1]
    a = regroup(rel[...])
    for n, (lo, hi) in enumerate(tiles(width)):
        g = jnp.concatenate([r[:, lo:hi] for r in (g0, g1, g2, g3)], axis=0)
        term = nt(g, eff[:, lo:hi])
        m = (tn(a, g) * base[:, lo:hi].astype(F32)).astype(BF16)
        lp, rp = factor_sums(m, left[...], right[:, lo:hi])
        rpart[:, lo:hi] = rp
        if n == 0:
            acc[...] = term
            lpart[...] = lp
        else:
            acc[...] += term
            lpart[...] += lp
    total = (regroup(acc[...]) + gi[...]).astype(BF16)
    y, x, core = ids[0], ids[1], ids[3]
    for dx in range(4):
        for dy in range(4):
            block = lax.rem(y + dy, 4) * 4 + lax.rem(x + dx, 4)
            at = (dx * 4 + dy) * 32
            piece = total[at : at + 32]
            mine = lax.rem(block, 2) == core

            @pl.when(mine)
            def _():
                own[block // 2] = piece

            @pl.when(jnp.logical_not(mine))
            def _():
                other[block // 2] = piece


def down_grad_body(ids, hid, cot, base, left, right, lpart, rpart):
    c = cot[...]
    for n, (lo, hi) in enumerate(tiles(base.shape[0])):
        m = (tn(hid[:, lo:hi], c) * base[lo:hi, :].astype(F32)).astype(BF16)
        lp, rp = factor_sums(m, left[:, lo:hi], right[...])
        lpart[:, lo:hi] = lp
        if n == 0:
            rpart[...] = rp
        else:
            rpart[...] += rp


def scatter4(chunks, axis):
    return chunks[0], shift(chunks[1], axis, 1), shift(chunks[2], axis, 2), shift(chunks[3], axis, -1)


def gather4(v, axis):
    return v, shift(v, axis, -1), shift(v, axis, -2), shift(v, axis, 1)


def scatter16(chunks, first, second):
    got = scatter4(chunks, first)
    parts = [add_all(*[g[32 * k : 32 * k + 32] for g in got]) for k in range(4)]
    return add_all(*scatter4([parts[0]] + [p.astype(BF16) for p in parts[1:]], second))


def gather16(v, first, second):
    return gather4(jnp.concatenate(gather4(v, first), axis=0), second)


def to_all(v, axis):
    return lax.all_to_all(v, axis, split_axis=0, concat_axis=0, tiled=True)


def hilo(v):
    return jnp.concatenate(halves(v), axis=0)


def per_device(
    activations,
    cotangent,
    gate_base,
    up_base,
    down_base,
    gate_left,
    gate_right,
    up_left,
    up_right,
    down_left,
    down_right,
):
    y, x, z, core = (lax.axis_index(a) for a in ("y", "x", "z", "core"))
    ids = jnp.stack([y, x, z, core]).astype(jnp.int32)
    ff = gate_base.shape[1]
    dm = gate_base.shape[0]

    act_z = to_all(jnp.broadcast_to(activations[None], (NZ,) + activations.shape), "z")
    act_o = shift(act_z, "core", 1)
    first = core == 0
    act = jnp.stack([jnp.where(first, act_z, act_o), jnp.where(first, act_o, act_z)], axis=1)
    act = act.reshape(16, 32, dm)
    cot = to_all(jnp.broadcast_to(cotangent[None], (16,) + cotangent.shape), ROW)

    gate_eff = effective(gate_base, gate_left, gate_right)
    up_eff = effective(up_base, up_left, up_right)
    down_eff = effective(down_base, down_left, down_right)

    quarter = [((128, ff), F32)] + [((128, ff), BF16)] * 3
    flops = 2 * 512 * dm * ff
    *gate_c, rel = kernel_call(
        gate_body, ids, [act, gate_eff], quarter + [((512, dm), BF16)], flops=flops
    )
    up_c = kernel_call(up_body, ids, [rel, up_eff], quarter, flops=flops)
    h_own, h_other = kernel_call(
        hid_body,
        ids,
        [cot, down_eff],
        [((256, ff), BF16), ((256, ff), BF16)],
        scratch=[pltpu.VMEM((512, dm), BF16)],
        flops=flops,
    )
    h_pair = add_all(h_own, shift(h_other, "core", 1)).astype(BF16).reshape(NZ, 32, ff)
    h_parts = to_all(h_pair, "z")
    grad_h = jnp.sum(h_parts.astype(F32), axis=0).astype(BF16)
    grad_h = transpose_grid(grad_h).astype(F32)
    gate_z = scatter16(gate_c, "x", "y")
    up_z = scatter16(up_c, "y", "x")

    hidden, d_gate, d_up = swish_parts(gate_z, up_z, grad_h)
    hidden_all = lax.all_gather(transpose_grid(hidden), COL, axis=0, tiled=True)
    gate_g = gather16(d_gate, "y", "x")
    up_g = gather16(d_up, "x", "y")

    gi, gate_lp, gate_rp = kernel_call(
        gate_grad_body,
        ids,
        [*gate_g, rel, gate_base, gate_eff, hilo(gate_left), hilo(gate_right)],
        [((512, dm), F32), ((32, dm), F32), ((32, ff), F32)],
        flops=3 * flops,
    )
    gi_own, gi_other, up_lp, up_rp = kernel_call(
        up_grad_body,
        ids,
        [*up_g, rel, up_base, up_eff, hilo(up_left), hilo(up_right), gi],
        [((8, 32, dm), BF16), ((8, 32, dm), BF16), ((32, dm), F32), ((32, ff), F32)],
        scratch=[pltpu.VMEM((512, dm), F32)],
        flops=3 * flops,
    )
    down_lp, down_rp = kernel_call(
        down_grad_body,
        ids,
        [hidden_all, cot.reshape(512, dm), down_base, hilo(down_left), hilo(down_right)],
        [((32, ff), F32), ((32, dm), F32)],
        flops=2 * flops,
    )

    gi_pair = add_all(gi_own, shift(gi_other, "core", 1)).astype(BF16)
    gi_parts = to_all(gi_pair, "z")
    grad_input = jnp.sum(gi_parts.astype(F32), axis=0).astype(BF16)

    pad = 8 * 384 - 2 * dm - ff
    lcat = jnp.concatenate([gate_lp, up_lp, down_lp, jnp.zeros((32, pad), F32)], axis=1)
    lparts = to_all(lcat.reshape(32, NZ, 384).swapaxes(0, 1), "z")
    lsum = jnp.sum(lparts, axis=0)
    lsum = lsum + shift(lsum, "core", 1)
    lall = to_all(jnp.broadcast_to(lsum[None], (NZ, 32, 384)), "z")
    lall = lall.swapaxes(0, 1).reshape(32, NZ * 384)
    gate_l, up_l, down_l = lall[:, :dm], lall[:, dm : 2 * dm], lall[:, 2 * dm : 2 * dm + ff]

    rcat = jnp.concatenate([gate_rp, up_rp, down_rp], axis=1).reshape(4, 8, -1)
    rrel = lax.dynamic_slice_in_dim(jnp.concatenate([rcat, rcat], axis=0), x, 4, axis=0)
    rsum = add_all(*scatter4([rrel[k] for k in range(4)], "x"))
    rsum = add_all(*gather4(rsum, "y"))
    rall = jnp.stack(gather4(rsum, "x"))
    rall = lax.dynamic_slice_in_dim(jnp.concatenate([rall, rall], axis=0), lax.rem(4 - x, 4), 4, axis=0)
    rall = rall.reshape(32, -1)
    gate_r, up_r, down_r = rall[:, :ff], rall[:, ff : 2 * ff], rall[:, 2 * ff :]
    return (grad_input, gate_l, gate_r, up_l, up_r, down_l, down_r)


def solution(mesh):
    fine = Mesh(mesh.devices.reshape(NY, NX, NZ, NC), ("y", "x", "z", "core"))
    both, left, right = P(ROW, COL), P(None, ROW), P(None, COL)
    return jax.shard_map(
        per_device,
        mesh=fine,
        in_specs=(P(COL, ROW), both, both, both, both, left, right, left, right, left, right),
        out_specs=(P(COL, ROW), left, right, left, right, left, right),
        check_vma=False,
    )
```

```python
import jax
import jax.numpy as jnp
from jax import lax
from jax.experimental import pallas as pl
from jax.experimental.pallas import tpu as pltpu
from jax.sharding import Mesh, PartitionSpec as P

F32 = jnp.float32
BF16 = jnp.bfloat16
NY, NX, NZ, NC = 4, 4, 8, 2
ROW = ("y", "x")
COL = ("z", "core")
TILE = 256
LANES = 128
VMEM_LIMIT = 48 * 1024 * 1024
BITREV = (0, 4, 2, 6, 1, 5, 3, 7)


def tiles(width):
    return [(at, min(at + TILE, width)) for at in range(0, width, TILE)]


def kernel_call(body, ids, args, outs, scratch=()):
    return pl.pallas_call(
        body,
        out_shape=[jax.ShapeDtypeStruct(s, d) for s, d in outs],
        in_specs=[pl.BlockSpec(memory_space=pltpu.SMEM)] + [pl.BlockSpec(memory_space=pltpu.VMEM)] * len(args),
        out_specs=[pl.BlockSpec(memory_space=pltpu.VMEM)] * len(outs),
        scratch_shapes=list(scratch),
        compiler_params=pltpu.CompilerParams(vmem_limit_bytes=VMEM_LIMIT),
        cost_estimate=pl.CostEstimate(flops=1024, bytes_accessed=1024, transcendentals=0),
    )(ids, *args)


def plane_permute(v, move, primary):
    perm = []
    for y in range(NY):
        for x in range(NX):
            for core in range(NC):
                on_x = (core == 0) == primary
                ty, tx = (y, move(x)) if on_x else (move(y), x)
                perm.append(((y * NX + x) * NC + core, (ty * NX + tx) * NC + core))
    return lax.ppermute(v, ("y", "x", "core"), perm)


def plane_shift(v, step, primary):
    return plane_permute(v, lambda i: (i + step) % 4, primary)


def z_swap(v, mask):
    return lax.ppermute(v, "z", [(i, i ^ mask) for i in range(NZ)])


def core_swap(v):
    return lax.ppermute(v, "core", [(0, 1), (1, 0)])


def to_columns(v):
    perm = [(j * 16 + b, (b ^ j) * 16 + j) for j in range(16) for b in range(16)]
    return lax.ppermute(v, ("y", "x", "z", "core"), perm)


def to_rows(v):
    perm = [(a * 16 + j, j * 16 + (a ^ j)) for a in range(16) for j in range(16)]
    return lax.ppermute(v, ("y", "x", "z", "core"), perm)


def to_all(v, axis):
    return lax.all_to_all(v, axis, split_axis=0, concat_axis=0, tiled=True)


def add_all(*vs):
    total = vs[0].astype(F32)
    for v in vs[1:]:
        total = total + v.astype(F32)
    return total


def swish_parts(gate_z, up_z, grad_h):
    squash = jax.nn.sigmoid(gate_z)
    swished = gate_z * squash
    hidden = (swished * up_z).astype(BF16)
    d_up = (grad_h * swished).astype(BF16)
    d_gate = (grad_h * up_z * squash * (1.0 + gate_z * (1.0 - squash))).astype(BF16)
    return hidden, d_gate, d_up


def nt(a, b):
    return lax.dot_general(a, b, (((1,), (1,)), ((), ())), preferred_element_type=F32)


def tn(a, b):
    return lax.dot_general(a, b, (((0,), (0,)), ((), ())), preferred_element_type=F32)


def nn(a, b):
    return jnp.dot(a, b, preferred_element_type=F32)


def split(v):
    high = v.astype(BF16)
    return high, (v - high.astype(F32)).astype(BF16)


def hilo(v):
    return jnp.concatenate(split(v), axis=0)


def plane_block(ids, at):
    y, x, z, core = ids[0], ids[1], ids[2], ids[3]
    one, two = at // 4, at % 4
    dx = jnp.where(core == 0, one, two)
    dy = jnp.where(core == 0, two, one)
    return (((y + dy) & 3) * 4 + ((x + dx) & 3)) ^ (z * 2 + core)


def slot_of(off):
    return ((off & 1) << 2) | (off & 2) | (off >> 2)


def eff_body(ids, *refs):
    n = len(refs) // 4
    for base, wide, narrow, eff in zip(refs[:n], refs[n : 2 * n], refs[2 * n : 3 * n], refs[3 * n :]):
        nh, nl = split(narrow[...])
        n3 = jnp.concatenate([nh, nh, nl], axis=0)
        for lo, hi in tiles(base.shape[0]):
            wh, wl = split(wide[:, lo:hi])
            lowrank = tn(jnp.concatenate([wh, wl, wh], axis=0), n3)
            eff[lo:hi, :] = (base[lo:hi, :].astype(F32) * (1.0 + lowrank)).astype(BF16)


def hid_body(ids, cot, eff, own, other, rel):
    core = ids[3]
    for k in range(2):
        for n in range(8):
            at = (k * 8 + n) * 32
            rel[at : at + 32, :] = cot[n * 2 + (core ^ k)]
    a = rel[...]
    for lo, hi in tiles(eff.shape[0]):
        r = nt(a, eff[lo:hi, :])
        own[:, :, lo:hi] = r[:256].reshape(8, 32, hi - lo).astype(BF16)
        other[:, :, lo:hi] = r[256:].reshape(8, 32, hi - lo).astype(BF16)


def sum_body(ids, act_own, act_other, gate_eff, up_eff, c0, c1, c2, c3, rel, act):
    z, core = ids[2], ids[3]
    act[core] = act_own[...]
    act[1 - core] = act_other[...]
    for at in range(16):
        block = plane_block(ids, at)
        rel[at * 32 : at * 32 + 32, :] = act[block & 1, slot_of((block >> 1) ^ z)]
    a = rel[...]
    for m, eff in enumerate((gate_eff, up_eff)):
        for lo, hi in tiles(eff.shape[0]):
            r = nt(a, eff[lo:hi, :])
            for k, out in enumerate((c0, c1, c2, c3)):
                part = r[k * 128 : (k + 1) * 128].reshape(4, 32, hi - lo)
                out[:, m, :, lo:hi] = part.astype(out.dtype)


def store_tiles(out, start, blocks, lane, v):
    width = v.shape[1]
    pad = -width % LANES
    if pad:
        v = jnp.concatenate([v, jnp.zeros((32, pad), F32)], axis=1)
    for j in range(v.shape[1] // LANES):
        for g in range(4):
            out[start + g * blocks + lane // LANES + j] = v[g * 8 : g * 8 + 8, j * LANES : (j + 1) * LANES]


def load_tiles(v, start, width):
    blocks = -(-width // LANES)
    v = v[start : start + 4 * blocks].reshape(4, blocks, 8, LANES)
    return v.swapaxes(1, 2).reshape(32, blocks * LANES)[:, :width]


def grad_body(ids, g0, g1, g2, g3, rel, *refs):
    bases, effs, wides, narrows = refs[0:2], refs[2:4], refs[4:6], refs[6:8]
    gi, left, right, acc = refs[8:]
    a = rel[...]
    dm = rel.shape[1]
    for m in range(2):
        base, eff, wide, narrow = bases[m], effs[m], wides[m], narrows[m]
        width = base.shape[0]
        blocks = -(-width // LANES)
        n2 = hilo(narrow[...])
        total = jnp.zeros((64, dm), F32)
        for n, (lo, hi) in enumerate(tiles(width)):
            g = jnp.concatenate([r[:, m, :, lo:hi].reshape(128, hi - lo) for r in (g0, g1, g2, g3)], axis=0)
            term = nn(g, eff[lo:hi, :])
            masked = (tn(g, a) * base[lo:hi, :].astype(F32)).astype(BF16)
            rp = nt(n2, masked)
            total = total + nn(hilo(wide[:, lo:hi]), masked)
            store_tiles(right, m * 4 * blocks, blocks, lo, rp[:32] + rp[32:])
            if n == 0 and m == 0:
                acc[...] = term
            else:
                acc[...] += term
        store_tiles(left, m * dm // 32, dm // LANES, 0, total[:32] + total[32:])
    z, core = ids[2], ids[3]
    for at in range(16):
        block = plane_block(ids, at)
        slot = slot_of((block >> 1) ^ z)
        for g in range(4):
            row = at * 32 + g * 8
            for j in range(dm // LANES):
                piece = acc[row : row + 8, j * LANES : (j + 1) * LANES]
                gi[(block & 1) ^ core, slot, g * (dm // LANES) + j] = piece


def down_grad_body(ids, hid_own, hid_other, cot, base, wide, narrow, left, right, rel):
    core = ids[3]
    for k in range(2):
        for n in range(8):
            at = (k * 8 + n) * 32
            rel[at : at + 32, :] = cot[n * 2 + (core ^ k)]
    c = rel[...]
    n2 = hilo(narrow[...])
    width, dm = base.shape
    blocks = -(-width // LANES)
    total = jnp.zeros((64, dm), F32)
    for lo, hi in tiles(width):
        h = jnp.concatenate([r[:, :, lo:hi].reshape(256, hi - lo) for r in (hid_own, hid_other)], axis=0)
        masked = (tn(h, c) * base[lo:hi, :].astype(F32)).astype(BF16)
        lp = nt(n2, masked)
        total = total + nn(hilo(wide[:, lo:hi]), masked)
        store_tiles(left, 0, blocks, lo, lp[:32] + lp[32:])
    store_tiles(right, 0, dm // LANES, 0, total[:32] + total[32:])


def scatter4(chunks, primary):
    return [chunks[0]] + [plane_shift(chunks[k], k, primary) for k in (1, 2, 3)]


def gather4(v, primary):
    return [v] + [plane_shift(v, -k, primary) for k in (1, 2, 3)]


def per_device(
    activations,
    cotangent,
    gate_base,
    up_base,
    down_base,
    gate_left,
    gate_right,
    up_left,
    up_right,
    down_left,
    down_right,
):
    ids = jnp.stack([lax.axis_index(a) for a in ("y", "x", "z", "core")]).astype(jnp.int32)
    dm, ff = gate_base.shape
    gate_t, up_t = gate_base.T, up_base.T

    cot = to_all(jnp.broadcast_to(cotangent[None], (16,) + cotangent.shape), ROW)
    act_own = activations[None]
    for mask in (4, 2, 1):
        act_own = jnp.concatenate([act_own, z_swap(act_own, mask)], axis=0)
    (down_eff,) = kernel_call(eff_body, ids, [down_base, down_left, down_right], [((ff, dm), BF16)])
    ids, act_own = lax.optimization_barrier((ids, act_own))
    act_other = core_swap(act_own)
    gate_eff, up_eff = kernel_call(
        eff_body, ids, [gate_t, up_t, gate_right, up_right, gate_left, up_left], [((ff, dm), BF16)] * 2
    )
    h_own, h_other = kernel_call(
        hid_body,
        ids,
        [cot, down_eff],
        [((8, 32, ff), BF16)] * 2,
        scratch=[pltpu.VMEM((512, dm), BF16)],
    )
    h_pair = add_all(h_own, core_swap(h_other)).astype(BF16)
    act_own, act_other, h_pair = lax.optimization_barrier((act_own, act_other, h_pair))
    *chunks, act_rel = kernel_call(
        sum_body,
        ids,
        [act_own, act_other, gate_eff, up_eff],
        [((4, 2, 32, ff), BF16)] * 4 + [((512, dm), BF16)],
        scratch=[pltpu.VMEM((2, 8, 32, dm), BF16)],
    )
    grad_h = jnp.sum(to_all(h_pair, "z").astype(F32), axis=0)
    grad_h = to_columns(grad_h.astype(BF16)).astype(F32)

    got = scatter4(chunks, True)
    parts = [add_all(*[g[k] for g in got]) for k in range(4)]
    zs = add_all(*scatter4([parts[0]] + [p.astype(BF16) for p in parts[1:]], False))

    hidden, d_gate, d_up = swish_parts(zs[0], zs[1], grad_h)
    hid = to_rows(hidden)
    near = jnp.stack(gather4(jnp.stack([d_gate, d_up]), False))
    near, hid = lax.optimization_barrier((near, hid))
    grads = gather4(near, True)
    hid_own = to_all(jnp.broadcast_to(hid[None], (NZ,) + hid.shape), "z")
    hid_other = core_swap(hid_own)

    wide_tiles, narrow_tiles = 4 * -(-ff // LANES), dm // 32
    gi, l_up, r_up = kernel_call(
        grad_body,
        ids,
        [*grads, act_rel, gate_t, up_t, gate_eff, up_eff, gate_right, up_right, gate_left, up_left],
        [
            ((2, 8, narrow_tiles, 8, LANES), F32),
            ((2 * narrow_tiles, 8, LANES), F32),
            ((2 * wide_tiles, 8, LANES), F32),
        ],
        scratch=[pltpu.VMEM((512, dm), F32)],
    )
    l_down, r_down = kernel_call(
        down_grad_body,
        ids,
        [hid_own, hid_other, cot, down_base, down_left, down_right],
        [((wide_tiles, 8, LANES), F32), ((narrow_tiles, 8, LANES), F32)],
        scratch=[pltpu.VMEM((512, dm), BF16)],
    )

    r_all = jnp.concatenate([r_up, r_down], axis=0)
    for primary in (True, False):
        r_all = r_all + add_all(*gather4(r_all.astype(BF16), primary)[1:])

    first = lax.axis_index("core") == 0
    l_all = jnp.concatenate([l_up, l_down], axis=0)
    half = l_all.shape[0] // 2
    low, high = l_all[:half], l_all[half:]
    mine, theirs = jnp.where(first, low, high), jnp.where(first, high, low)
    n = 8 * gi.shape[2]
    both = core_swap(jnp.concatenate([gi[1].reshape(n, 8, LANES), theirs], axis=0))
    gi, l_sum = gi[0].reshape(n, 8, LANES) + both[:n], mine + both[n:]
    for mask in (1, 2, 4):
        n = n // 2
        both = z_swap(jnp.concatenate([gi[n:], l_sum], axis=0).astype(BF16), mask).astype(F32)
        gi, l_sum = gi[:n] + both[:n], l_sum + both[n:]
    grad_input = load_tiles(gi, 0, dm).astype(BF16)
    l_other = core_swap(l_sum)
    l_all = jnp.concatenate([jnp.where(first, l_sum, l_other), jnp.where(first, l_other, l_sum)], axis=0)
    gate_l = load_tiles(l_all, 0, dm)
    up_l = load_tiles(l_all, narrow_tiles, dm)
    down_l = load_tiles(l_all, 2 * narrow_tiles, ff)
    gate_r = load_tiles(r_all, 0, ff)
    up_r = load_tiles(r_all, wide_tiles, ff)
    down_r = load_tiles(r_all, 2 * wide_tiles, dm)
    return (grad_input, gate_l, gate_r, up_l, up_r, down_l, down_r)


def solution(mesh):
    fine = Mesh(mesh.devices.reshape(NY, NX, NZ, NC), ("y", "x", "z", "core"))
    both, left, right = P(ROW, COL), P(None, ROW), P(None, COL)
    return jax.shard_map(
        per_device,
        mesh=fine,
        in_specs=(P(COL, ROW), both, both, both, both, left, right, left, right, left, right),
        out_specs=(P(COL, ROW), left, right, left, right, left, right),
        check_vma=False,
    )
```

```python
import jax
import jax.numpy as jnp
from jax import lax
from jax.experimental import pallas as pl
from jax.experimental.pallas import tpu as pltpu
from jax.sharding import Mesh, PartitionSpec as P

F32 = jnp.float32
BF16 = jnp.bfloat16
NY, NX, NZ, NC = 4, 4, 8, 2
ROW = ("y", "x")
COL = ("z", "core")
TILE = 256
LANES = 128
MIB = 1024 * 1024
BITREV = (0, 4, 2, 6, 1, 5, 3, 7)


def tiles(width):
    return [(at, min(at + TILE, width)) for at in range(0, width, TILE)]


def kernel_call(body, ids, args, outs, scratch=(), raw=0, limit=32):
    return pl.pallas_call(
        body,
        out_shape=[jax.ShapeDtypeStruct(s, d) for s, d in outs],
        in_specs=[pl.BlockSpec(memory_space=pltpu.SMEM)] + [pl.BlockSpec(memory_space=pl.ANY)] * raw
        + [pl.BlockSpec(memory_space=pltpu.VMEM)] * (len(args) - raw),
        out_specs=[pl.BlockSpec(memory_space=pltpu.VMEM)] * len(outs),
        scratch_shapes=list(scratch),
        compiler_params=pltpu.CompilerParams(vmem_limit_bytes=limit * MIB),
        cost_estimate=pl.CostEstimate(flops=1024, bytes_accessed=1024, transcendentals=0),
    )(ids, *args)


def plane_permute(v, move, primary):
    perm = []
    for y in range(NY):
        for x in range(NX):
            for core in range(NC):
                on_x = (core == 0) == primary
                ty, tx = (y, move(x)) if on_x else (move(y), x)
                perm.append(((y * NX + x) * NC + core, (ty * NX + tx) * NC + core))
    return lax.ppermute(v, ("y", "x", "core"), perm)


def plane_shift(v, step, primary):
    return plane_permute(v, lambda i: (i + step) % 4, primary)


def z_swap(v, mask):
    return lax.ppermute(v, "z", [(i, i ^ mask) for i in range(NZ)])


def core_swap(v):
    return lax.ppermute(v, "core", [(0, 1), (1, 0)])


MOVES = (
    (3, 2), (2, 2), (2, 0), (2, 1), (1, 1), (3, 3), (0, 3), (1, 0),
    (0, 0), (0, 1), (3, 0), (0, 2), (1, 3), (3, 1), (2, 3), (1, 2),
)


def grid_pairs():
    pairs = []
    for j in range(16):
        for b in range(16):
            oy, ox = MOVES[(b - (j & 14)) & 15]
            a = (((j >> 2) + oy) & 3) * 4 + (((j & 3) + ox) & 3)
            pairs.append((j * 16 + b, a * 16 + j))
    return pairs


def to_columns(v):
    return lax.ppermute(v, ("y", "x", "z", "core"), grid_pairs())


def to_rows(v):
    return lax.ppermute(v, ("y", "x", "z", "core"), [(b, a) for a, b in grid_pairs()])


def move_table():
    words = [0, 0]
    for source, (oy, ox) in enumerate(MOVES):
        at = oy * 4 + ox
        words[at // 8] |= source << (4 * (at % 8))
    return [w - (1 << 32) if w >= 1 << 31 else w for w in words]


def to_all(v, axis):
    return lax.all_to_all(v, axis, split_axis=0, concat_axis=0, tiled=True)


def add_all(*vs):
    total = vs[0].astype(F32)
    for v in vs[1:]:
        total = total + v.astype(F32)
    return total


def swish_parts(gate_z, up_z, grad_h):
    squash = jax.nn.sigmoid(gate_z)
    swished = gate_z * squash
    hidden = (swished * up_z).astype(BF16)
    d_up = (grad_h * swished).astype(BF16)
    d_gate = (grad_h * up_z * squash * (1.0 + gate_z * (1.0 - squash))).astype(BF16)
    return hidden, d_gate, d_up


def nt(a, b):
    return lax.dot_general(a, b, (((1,), (1,)), ((), ())), preferred_element_type=F32)


def tn(a, b):
    return lax.dot_general(a, b, (((0,), (0,)), ((), ())), preferred_element_type=F32)


def nn(a, b):
    return jnp.dot(a, b, preferred_element_type=F32)


def split(v):
    high = v.astype(BF16)
    return high, (v - high.astype(F32)).astype(BF16)


def hilo(v):
    return jnp.concatenate(split(v), axis=0)


def plane_block(ids, at):
    y, x, z, core = ids[0], ids[1], ids[2], ids[3]
    one, two = at // 4, at % 4
    dx = jnp.where(core == 0, one, two)
    dy = jnp.where(core == 0, two, one)
    unit = z * 2 + core
    oy, ox = (y + dy - (unit >> 2)) & 3, (x + dx - (unit & 3)) & 3
    low, high = move_table()
    word = jnp.where(oy < 2, jnp.int32(low), jnp.int32(high))
    source = lax.shift_right_logical(word, ((oy & 1) * 4 + ox) * 4) & 15
    return ((z * 2 + (source & 14)) & 15) | (source & 1)


def slot_of(off):
    return ((off & 1) << 2) | (off & 2) | (off >> 2)


def eff_body(ids, *refs):
    n = len(refs) // 4
    for base, wide, narrow, eff in zip(refs[:n], refs[n : 2 * n], refs[2 * n : 3 * n], refs[3 * n :]):
        nh, nl = split(narrow[...])
        n3 = jnp.concatenate([nh, nh, nl], axis=0)
        for lo, hi in tiles(base.shape[0]):
            wh, wl = split(wide[:, lo:hi])
            lowrank = tn(jnp.concatenate([wh, wl, wh], axis=0), n3)
            eff[lo:hi, :] = (base[lo:hi, :].astype(F32) * (1.0 + lowrank)).astype(BF16)


def hid_body(ids, cot, eff, own, other, rel):
    core = ids[3]
    for k in range(2):
        for n in range(8):
            at = (k * 8 + n) * 32
            rel[at : at + 32, :] = cot[n * 2 + (core ^ k)]
    a = rel[...]
    for lo, hi in tiles(eff.shape[0]):
        r = nt(a, eff[lo:hi, :])
        own[:, :, lo:hi] = r[:256].reshape(8, 32, hi - lo).astype(BF16)
        other[:, :, lo:hi] = r[256:].reshape(8, 32, hi - lo).astype(BF16)


def sum_body(ids, act_own, act_other, gate_eff, up_eff, c0, c1, c2, c3, rel, act):
    z, core = ids[2], ids[3]
    act[core] = act_own[...]
    act[1 - core] = act_other[...]
    for at in range(16):
        block = plane_block(ids, at)
        rel[at * 32 : at * 32 + 32, :] = act[block & 1, slot_of((block >> 1) ^ z)]
    a = rel[...]
    for m, eff in enumerate((gate_eff, up_eff)):
        for lo, hi in tiles(eff.shape[0]):
            r = nt(a, eff[lo:hi, :])
            for k, out in enumerate((c0, c1, c2, c3)):
                part = r[k * 128 : (k + 1) * 128].reshape(4, 32, hi - lo)
                out[:, m, :, lo:hi] = part.astype(out.dtype)


def store_tiles(out, start, blocks, lane, v):
    width = v.shape[1]
    pad = -width % LANES
    if pad:
        v = jnp.concatenate([v, jnp.zeros((32, pad), F32)], axis=1)
    for j in range(v.shape[1] // LANES):
        for g in range(4):
            out[start + g * blocks + lane // LANES + j] = v[g * 8 : g * 8 + 8, j * LANES : (j + 1) * LANES]


def load_tiles(v, start, width):
    blocks = -(-width // LANES)
    v = v[start : start + 4 * blocks].reshape(4, blocks, 8, LANES)
    return v.swapaxes(1, 2).reshape(32, blocks * LANES)[:, :width]


def grad_body(ids, gate_base, gate_eff, up_base, up_eff, g0, g1, g2, g3, rel, *refs):
    wides, narrows = refs[0:2], refs[2:4]
    gi, left, right, acc, weights, sems = refs[4:]
    copies = [
        pltpu.make_async_copy(src, weights.at[k], sems.at[k])
        for k, src in enumerate((gate_eff, up_eff, gate_base, up_base))
    ]
    for copy in copies:
        copy.start()
    width, dm = weights.shape[1:]
    blocks = -(-width // LANES)

    def tile(m, lo, hi):
        return jnp.concatenate([r[:, m, :, lo:hi].reshape(128, hi - lo) for r in (g0, g1, g2, g3)], axis=0)

    for m in range(2):
        copies[m].wait()
        for n, (lo, hi) in enumerate(tiles(width)):
            term = nn(tile(m, lo, hi), weights[m, lo:hi, :])
            if n == 0 and m == 0:
                acc[...] = term
            else:
                acc[...] += term
    a = rel[...]
    for m in range(2):
        copies[2 + m].wait()
        n2 = hilo(narrows[m][...])
        total = jnp.zeros((64, dm), F32)
        for lo, hi in tiles(width):
            masked = (tn(tile(m, lo, hi), a) * weights[2 + m, lo:hi, :].astype(F32)).astype(BF16)
            rp = nt(n2, masked)
            total = total + nn(hilo(wides[m][:, lo:hi]), masked)
            store_tiles(right, m * 4 * blocks, blocks, lo, rp[:32] + rp[32:])
        store_tiles(left, m * dm // 32, dm // LANES, 0, total[:32] + total[32:])
    z, core = ids[2], ids[3]
    for at in range(16):
        block = plane_block(ids, at)
        slot = slot_of((block >> 1) ^ z)
        for g in range(4):
            row = at * 32 + g * 8
            for j in range(dm // LANES):
                piece = acc[row : row + 8, j * LANES : (j + 1) * LANES]
                gi[(block & 1) ^ core, slot, g * (dm // LANES) + j] = piece


def down_grad_body(ids, hid_own, hid_other, cot, base, wide, narrow, left, right, rel):
    core = ids[3]
    for k in range(2):
        for n in range(8):
            at = (k * 8 + n) * 32
            rel[at : at + 32, :] = cot[n * 2 + (core ^ k)]
    c = rel[...]
    n2 = hilo(narrow[...])
    width, dm = base.shape
    blocks = -(-width // LANES)
    total = jnp.zeros((64, dm), F32)
    for lo, hi in tiles(width):
        h = jnp.concatenate([r[:, :, lo:hi].reshape(256, hi - lo) for r in (hid_own, hid_other)], axis=0)
        masked = (tn(h, c) * base[lo:hi, :].astype(F32)).astype(BF16)
        lp = nt(n2, masked)
        total = total + nn(hilo(wide[:, lo:hi]), masked)
        store_tiles(left, 0, blocks, lo, lp[:32] + lp[32:])
    store_tiles(right, 0, dm // LANES, 0, total[:32] + total[32:])


def scatter4(chunks, primary):
    return [chunks[0]] + [plane_shift(chunks[k], k, primary) for k in (1, 2, 3)]


def gather4(v, primary):
    return [v] + [plane_shift(v, -k, primary) for k in (1, 2, 3)]


def per_device(
    activations,
    cotangent,
    gate_base,
    up_base,
    down_base,
    gate_left,
    gate_right,
    up_left,
    up_right,
    down_left,
    down_right,
):
    ids = jnp.stack([lax.axis_index(a) for a in ("y", "x", "z", "core")]).astype(jnp.int32)
    dm, ff = gate_base.shape
    gate_t, up_t = gate_base.T, up_base.T

    cot = to_all(jnp.broadcast_to(cotangent[None], (16,) + cotangent.shape), ROW)
    act_own = activations[None]
    for mask in (4, 2, 1):
        act_own = jnp.concatenate([act_own, z_swap(act_own, mask)], axis=0)
    (down_eff,) = kernel_call(eff_body, ids, [down_base, down_left, down_right], [((ff, dm), BF16)])
    ids, act_own = lax.optimization_barrier((ids, act_own))
    act_other = core_swap(act_own)
    gate_eff, up_eff = kernel_call(
        eff_body, ids, [gate_t, up_t, gate_right, up_right, gate_left, up_left], [((ff, dm), BF16)] * 2
    )
    h_own, h_other = kernel_call(
        hid_body,
        ids,
        [cot, down_eff],
        [((8, 32, ff), BF16)] * 2,
        scratch=[pltpu.VMEM((512, dm), BF16)],
    )
    h_pair = add_all(h_own, core_swap(h_other)).astype(BF16)
    act_own, act_other, h_pair = lax.optimization_barrier((act_own, act_other, h_pair))
    *chunks, act_rel = kernel_call(
        sum_body,
        ids,
        [act_own, act_other, gate_eff, up_eff],
        [((4, 2, 32, ff), BF16)] * 4 + [((512, dm), BF16)],
        scratch=[pltpu.VMEM((2, 8, 32, dm), BF16)],
    )
    grad_h = jnp.sum(to_all(h_pair, "z").astype(F32), axis=0)
    grad_h = to_columns(grad_h.astype(BF16)).astype(F32)

    got = scatter4(chunks, True)
    parts = [add_all(*[g[k] for g in got]).astype(BF16) for k in range(4)]
    zs = add_all(*scatter4(parts, False))

    hidden, d_gate, d_up = swish_parts(zs[0], zs[1], grad_h)
    hid = to_rows(hidden)
    near = jnp.stack(gather4(jnp.stack([d_gate, d_up]), False))
    near, hid = lax.optimization_barrier((near, hid))
    grads = gather4(near, True)
    hid_own = to_all(jnp.broadcast_to(hid[None], (NZ,) + hid.shape), "z")
    hid_other = core_swap(hid_own)

    wide_tiles, narrow_tiles = 4 * -(-ff // LANES), dm // 32
    gi, l_up, r_up = kernel_call(
        grad_body,
        ids,
        [gate_t, gate_eff, up_t, up_eff, *grads, act_rel, gate_right, up_right, gate_left, up_left],
        [
            ((2, 8, narrow_tiles, 8, LANES), F32),
            ((2 * narrow_tiles, 8, LANES), F32),
            ((2 * wide_tiles, 8, LANES), F32),
        ],
        scratch=[pltpu.VMEM((512, dm), F32), pltpu.VMEM((4, ff, dm), BF16), pltpu.SemaphoreType.DMA((4,))],
        raw=4,
        limit=60,
    )
    l_down, r_down = kernel_call(
        down_grad_body,
        ids,
        [hid_own, hid_other, cot, down_base, down_left, down_right],
        [((wide_tiles, 8, LANES), F32), ((narrow_tiles, 8, LANES), F32)],
        scratch=[pltpu.VMEM((512, dm), BF16)],
        limit=60,
    )

    r_all = jnp.concatenate([r_up, r_down], axis=0)
    for primary in (True, False):
        r_all = r_all + add_all(*gather4(r_all.astype(BF16), primary)[1:])

    first = lax.axis_index("core") == 0
    l_all = jnp.concatenate([l_up, l_down], axis=0)
    half = l_all.shape[0] // 2
    low, high = l_all[:half], l_all[half:]
    mine, theirs = jnp.where(first, low, high), jnp.where(first, high, low)
    n = 8 * gi.shape[2]
    both = core_swap(jnp.concatenate([gi[1].reshape(n, 8, LANES), theirs], axis=0))
    gi, l_sum = gi[0].reshape(n, 8, LANES) + both[:n], mine + both[n:]
    for mask in (1, 2, 4):
        n = n // 2
        both = z_swap(jnp.concatenate([gi[n:], l_sum], axis=0).astype(BF16), mask).astype(F32)
        gi, l_sum = gi[:n] + both[:n], l_sum + both[n:]
    grad_input = load_tiles(gi, 0, dm).astype(BF16)
    l_other = core_swap(l_sum)
    l_all = jnp.concatenate([jnp.where(first, l_sum, l_other), jnp.where(first, l_other, l_sum)], axis=0)
    gate_l = load_tiles(l_all, 0, dm)
    up_l = load_tiles(l_all, narrow_tiles, dm)
    down_l = load_tiles(l_all, 2 * narrow_tiles, ff)
    gate_r = load_tiles(r_all, 0, ff)
    up_r = load_tiles(r_all, wide_tiles, ff)
    down_r = load_tiles(r_all, 2 * wide_tiles, dm)
    return (grad_input, gate_l, gate_r, up_l, up_r, down_l, down_r)


def solution(mesh):
    fine = Mesh(mesh.devices.reshape(NY, NX, NZ, NC), ("y", "x", "z", "core"))
    both, left, right = P(ROW, COL), P(None, ROW), P(None, COL)
    return jax.shard_map(
        per_device,
        mesh=fine,
        in_specs=(P(COL, ROW), both, both, both, both, left, right, left, right, left, right),
        out_specs=(P(COL, ROW), left, right, left, right, left, right),
        check_vma=False,
    )
```

```python
import jax
import jax.numpy as jnp
from jax import lax
from jax.experimental import pallas as pl
from jax.experimental.pallas import tpu as pltpu
from jax.sharding import Mesh, PartitionSpec as P

F32 = jnp.float32
BF16 = jnp.bfloat16
NY, NX, NZ, NC = 4, 4, 8, 2
ROW = ("y", "x")
COL = ("z", "core")
TILE = 256
LANES = 128
MIB = 1024 * 1024
BITREV = (0, 4, 2, 6, 1, 5, 3, 7)


def tiles(width):
    return [(at, min(at + TILE, width)) for at in range(0, width, TILE)]


def kernel_call(body, ids, args, outs, scratch=(), raw=0, limit=32):
    return pl.pallas_call(
        body,
        out_shape=[jax.ShapeDtypeStruct(s, d) for s, d in outs],
        in_specs=[pl.BlockSpec(memory_space=pltpu.SMEM)] + [pl.BlockSpec(memory_space=pl.ANY)] * raw
        + [pl.BlockSpec(memory_space=pltpu.VMEM)] * (len(args) - raw),
        out_specs=[pl.BlockSpec(memory_space=pltpu.VMEM)] * len(outs),
        scratch_shapes=list(scratch),
        compiler_params=pltpu.CompilerParams(vmem_limit_bytes=limit * MIB),
        cost_estimate=pl.CostEstimate(flops=1024, bytes_accessed=1024, transcendentals=0),
    )(ids, *args)


def plane_permute(v, move, primary):
    perm = []
    for y in range(NY):
        for x in range(NX):
            for core in range(NC):
                on_x = (core == 0) == primary
                ty, tx = (y, move(x)) if on_x else (move(y), x)
                perm.append(((y * NX + x) * NC + core, (ty * NX + tx) * NC + core))
    return lax.ppermute(v, ("y", "x", "core"), perm)


def plane_shift(v, step, primary):
    return plane_permute(v, lambda i: (i + step) % 4, primary)


def plane_swap(v, mask, primary):
    return plane_permute(v, lambda i: i ^ mask, primary)


def z_swap(v, mask):
    return lax.ppermute(v, "z", [(i, i ^ mask) for i in range(NZ)])


def core_swap(v):
    return lax.ppermute(v, "core", [(0, 1), (1, 0)])


MOVES = (
    (3, 2), (2, 2), (2, 0), (2, 1), (1, 1), (3, 3), (0, 3), (1, 0),
    (0, 0), (0, 1), (3, 0), (0, 2), (1, 3), (3, 1), (2, 3), (1, 2),
)


def grid_pairs():
    pairs = []
    for j in range(16):
        for b in range(16):
            oy, ox = MOVES[(b - (j & 14)) & 15]
            a = (((j >> 2) + oy) & 3) * 4 + (((j & 3) + ox) & 3)
            pairs.append((j * 16 + b, a * 16 + j))
    return pairs


def to_columns(v):
    return lax.ppermute(v, ("y", "x", "z", "core"), grid_pairs())


def to_rows(v):
    return lax.ppermute(v, ("y", "x", "z", "core"), [(b, a) for a, b in grid_pairs()])


def move_table():
    words = [0, 0]
    for source, (oy, ox) in enumerate(MOVES):
        at = oy * 4 + ox
        words[at // 8] |= source << (4 * (at % 8))
    return [w - (1 << 32) if w >= 1 << 31 else w for w in words]


def to_all(v, axis):
    return lax.all_to_all(v, axis, split_axis=0, concat_axis=0, tiled=True)


def add_all(*vs):
    total = vs[0].astype(F32)
    for v in vs[1:]:
        total = total + v.astype(F32)
    return total


def swish_parts(gate_z, up_z, grad_h):
    squash = jax.nn.sigmoid(gate_z)
    swished = gate_z * squash
    hidden = (swished * up_z).astype(BF16)
    d_up = (grad_h * swished).astype(BF16)
    d_gate = (grad_h * up_z * squash * (1.0 + gate_z * (1.0 - squash))).astype(BF16)
    return hidden, d_gate, d_up


def nt(a, b):
    return lax.dot_general(a, b, (((1,), (1,)), ((), ())), preferred_element_type=F32)


def tn(a, b):
    return lax.dot_general(a, b, (((0,), (0,)), ((), ())), preferred_element_type=F32)


def nn(a, b):
    return jnp.dot(a, b, preferred_element_type=F32)


def split(v):
    high = v.astype(BF16)
    return high, (v - high.astype(F32)).astype(BF16)


def hilo(v):
    return jnp.concatenate(split(v), axis=0)


def plane_block(ids, at):
    y, x, z, core = ids[0], ids[1], ids[2], ids[3]
    one, two = at // 4, at % 4
    dx = jnp.where(core == 0, one, two)
    dy = jnp.where(core == 0, two, one)
    unit = z * 2 + core
    oy, ox = (y + dy - (unit >> 2)) & 3, (x + dx - (unit & 3)) & 3
    low, high = move_table()
    word = jnp.where(oy < 2, jnp.int32(low), jnp.int32(high))
    source = lax.shift_right_logical(word, ((oy & 1) * 4 + ox) * 4) & 15
    return ((z * 2 + (source & 14)) & 15) | (source & 1)


def slot_of(off):
    return ((off & 1) << 2) | (off & 2) | (off >> 2)


def eff_body(ids, *refs):
    n = len(refs) // 4
    for base, wide, narrow, eff in zip(refs[:n], refs[n : 2 * n], refs[2 * n : 3 * n], refs[3 * n :]):
        nh, nl = split(narrow[...])
        n3 = jnp.concatenate([nh, nh, nl], axis=0)
        for lo, hi in tiles(base.shape[0]):
            wh, wl = split(wide[:, lo:hi])
            lowrank = tn(jnp.concatenate([wh, wl, wh], axis=0), n3)
            eff[lo:hi, :] = (base[lo:hi, :].astype(F32) * (1.0 + lowrank)).astype(BF16)


def hid_body(ids, cot, eff, own, other, rel):
    core = ids[3]
    for k in range(2):
        for n in range(8):
            at = (k * 8 + n) * 32
            rel[at : at + 32, :] = cot[n * 2 + (core ^ k)]
    a = rel[...]
    for lo, hi in tiles(eff.shape[0]):
        r = nt(a, eff[lo:hi, :])
        own[:, :, lo:hi] = r[:256].reshape(8, 32, hi - lo).astype(BF16)
        other[:, :, lo:hi] = r[256:].reshape(8, 32, hi - lo).astype(BF16)


def sum_body(ids, act_own, act_other, gate_eff, up_eff, c0, c1, c2, c3, rel, act):
    z, core = ids[2], ids[3]
    act[core] = act_own[...]
    act[1 - core] = act_other[...]
    for at in range(16):
        block = plane_block(ids, at)
        rel[at * 32 : at * 32 + 32, :] = act[block & 1, slot_of((block >> 1) ^ z)]
    a = rel[...]
    for m, eff in enumerate((gate_eff, up_eff)):
        for lo, hi in tiles(eff.shape[0]):
            r = nt(a, eff[lo:hi, :])
            for k, out in enumerate((c0, c1, c2, c3)):
                part = r[k * 128 : (k + 1) * 128].reshape(4, 32, hi - lo)
                out[:, m, :, lo:hi] = part.astype(out.dtype)


def store_tiles(out, start, blocks, lane, v):
    width = v.shape[1]
    pad = -width % LANES
    if pad:
        v = jnp.concatenate([v, jnp.zeros((32, pad), F32)], axis=1)
    for j in range(v.shape[1] // LANES):
        for g in range(4):
            out[start + g * blocks + lane // LANES + j] = v[g * 8 : g * 8 + 8, j * LANES : (j + 1) * LANES]


def load_tiles(v, start, width):
    blocks = -(-width // LANES)
    v = v[start : start + 4 * blocks].reshape(4, blocks, 8, LANES)
    return v.swapaxes(1, 2).reshape(32, blocks * LANES)[:, :width]


def grad_body(ids, gate_base, gate_eff, up_base, up_eff, g0, g1, g2, g3, rel, *refs):
    wides, narrows = refs[0:2], refs[2:4]
    gi, left, right, acc, weights, sems = refs[4:]
    copies = [
        pltpu.make_async_copy(src, weights.at[k], sems.at[k])
        for k, src in enumerate((gate_eff, up_eff, gate_base, up_base))
    ]
    for copy in copies:
        copy.start()
    width, dm = weights.shape[1:]
    blocks = -(-width // LANES)

    def tile(m, lo, hi):
        return jnp.concatenate([r[:, m, :, lo:hi].reshape(128, hi - lo) for r in (g0, g1, g2, g3)], axis=0)

    for m in range(2):
        copies[m].wait()
        for n, (lo, hi) in enumerate(tiles(width)):
            term = nn(tile(m, lo, hi), weights[m, lo:hi, :])
            if n == 0 and m == 0:
                acc[...] = term
            else:
                acc[...] += term
    a = rel[...]
    for m in range(2):
        copies[2 + m].wait()
        n2 = hilo(narrows[m][...])
        total = jnp.zeros((64, dm), F32)
        for lo, hi in tiles(width):
            masked = (tn(tile(m, lo, hi), a) * weights[2 + m, lo:hi, :].astype(F32)).astype(BF16)
            rp = nt(n2, masked)
            total = total + nn(hilo(wides[m][:, lo:hi]), masked)
            store_tiles(right, m * 4 * blocks, blocks, lo, rp[:32] + rp[32:])
        store_tiles(left, m * dm // 32, dm // LANES, 0, total[:32] + total[32:])
    z, core = ids[2], ids[3]
    for at in range(16):
        block = plane_block(ids, at)
        slot = slot_of((block >> 1) ^ z)
        for g in range(4):
            row = at * 32 + g * 8
            for j in range(dm // LANES):
                piece = acc[row : row + 8, j * LANES : (j + 1) * LANES]
                gi[(block & 1) ^ core, slot, g * (dm // LANES) + j] = piece


def down_grad_body(ids, hid_own, hid_other, cot, base, wide, narrow, left, right, rel):
    core = ids[3]
    for k in range(2):
        for n in range(8):
            at = (k * 8 + n) * 32
            rel[at : at + 32, :] = cot[n * 2 + (core ^ k)]
    c = rel[...]
    n2 = hilo(narrow[...])
    width, dm = base.shape
    blocks = -(-width // LANES)
    total = jnp.zeros((64, dm), F32)
    for lo, hi in tiles(width):
        h = jnp.concatenate([r[:, :, lo:hi].reshape(256, hi - lo) for r in (hid_own, hid_other)], axis=0)
        masked = (tn(h, c) * base[lo:hi, :].astype(F32)).astype(BF16)
        lp = nt(n2, masked)
        total = total + nn(hilo(wide[:, lo:hi]), masked)
        store_tiles(left, 0, blocks, lo, lp[:32] + lp[32:])
    store_tiles(right, 0, dm // LANES, 0, total[:32] + total[32:])


def scatter4(chunks, primary):
    return [chunks[0]] + [plane_shift(chunks[k], k, primary) for k in (1, 2, 3)]


def gather4(v, primary):
    return [v] + [plane_shift(v, -k, primary) for k in (1, 2, 3)]


def per_device(
    activations,
    cotangent,
    gate_base,
    up_base,
    down_base,
    gate_left,
    gate_right,
    up_left,
    up_right,
    down_left,
    down_right,
):
    ids = jnp.stack([lax.axis_index(a) for a in ("y", "x", "z", "core")]).astype(jnp.int32)
    dm, ff = gate_base.shape
    gate_t, up_t = gate_base.T, up_base.T

    cot = to_all(jnp.broadcast_to(cotangent[None], (16,) + cotangent.shape), ROW)
    act_own = activations[None]
    for mask in (4, 2, 1):
        act_own = jnp.concatenate([act_own, z_swap(act_own, mask)], axis=0)
    (down_eff,) = kernel_call(eff_body, ids, [down_base, down_left, down_right], [((ff, dm), BF16)])
    ids, act_own = lax.optimization_barrier((ids, act_own))
    act_other = core_swap(act_own)
    gate_eff, up_eff = kernel_call(
        eff_body, ids, [gate_t, up_t, gate_right, up_right, gate_left, up_left], [((ff, dm), BF16)] * 2
    )
    h_own, h_other = kernel_call(
        hid_body,
        ids,
        [cot, down_eff],
        [((8, 32, ff), BF16)] * 2,
        scratch=[pltpu.VMEM((512, dm), BF16)],
    )
    h_pair = add_all(h_own, core_swap(h_other)).astype(BF16)
    act_own, act_other, h_pair = lax.optimization_barrier((act_own, act_other, h_pair))
    *chunks, act_rel = kernel_call(
        sum_body,
        ids,
        [act_own, act_other, gate_eff, up_eff],
        [((4, 2, 32, ff), BF16)] * 4 + [((512, dm), BF16)],
        scratch=[pltpu.VMEM((2, 8, 32, dm), BF16)],
    )
    grad_h = jnp.sum(to_all(h_pair, "z").astype(F32), axis=0)
    grad_h = to_columns(grad_h.astype(BF16)).astype(F32)

    got = scatter4(chunks, True)
    parts = [add_all(*[g[k] for g in got]).astype(BF16) for k in range(4)]
    zs = add_all(*scatter4(parts, False))

    hidden, d_gate, d_up = swish_parts(zs[0], zs[1], grad_h)
    hid = to_rows(hidden)
    near = jnp.stack(gather4(jnp.stack([d_gate, d_up]), False))
    near, hid = lax.optimization_barrier((near, hid))
    grads = gather4(near, True)
    hid_own = to_all(jnp.broadcast_to(hid[None], (NZ,) + hid.shape), "z")
    hid_other = core_swap(hid_own)

    wide_tiles, narrow_tiles = 4 * -(-ff // LANES), dm // 32
    gi, l_up, r_up = kernel_call(
        grad_body,
        ids,
        [gate_t, gate_eff, up_t, up_eff, *grads, act_rel, gate_right, up_right, gate_left, up_left],
        [
            ((2, 8, narrow_tiles, 8, LANES), F32),
            ((2 * narrow_tiles, 8, LANES), F32),
            ((2 * wide_tiles, 8, LANES), F32),
        ],
        scratch=[pltpu.VMEM((512, dm), F32), pltpu.VMEM((4, ff, dm), BF16), pltpu.SemaphoreType.DMA((4,))],
        raw=4,
        limit=60,
    )
    l_down, r_down = kernel_call(
        down_grad_body,
        ids,
        [hid_own, hid_other, cot, down_base, down_left, down_right],
        [((wide_tiles, 8, LANES), F32), ((narrow_tiles, 8, LANES), F32)],
        scratch=[pltpu.VMEM((512, dm), BF16)],
        limit=60,
    )

    r_all = jnp.concatenate([r_up, r_down], axis=0)
    for primary in (True, False):
        for mask in (1, 2):
            r_all = r_all + plane_swap(r_all.astype(BF16), mask, primary).astype(F32)

    first = lax.axis_index("core") == 0
    l_all = jnp.concatenate([l_up, l_down], axis=0)
    half = l_all.shape[0] // 2
    low, high = l_all[:half], l_all[half:]
    mine, theirs = jnp.where(first, low, high), jnp.where(first, high, low)
    n = 8 * gi.shape[2]
    both = core_swap(jnp.concatenate([gi[1].reshape(n, 8, LANES), theirs], axis=0))
    gi, l_sum = gi[0].reshape(n, 8, LANES) + both[:n], mine + both[n:]
    for mask in (1, 2, 4):
        n = n // 2
        both = z_swap(jnp.concatenate([gi[n:], l_sum], axis=0).astype(BF16), mask).astype(F32)
        gi, l_sum = gi[:n] + both[:n], l_sum + both[n:]
    grad_input = load_tiles(gi, 0, dm).astype(BF16)
    l_other = core_swap(l_sum)
    l_all = jnp.concatenate([jnp.where(first, l_sum, l_other), jnp.where(first, l_other, l_sum)], axis=0)
    gate_l = load_tiles(l_all, 0, dm)
    up_l = load_tiles(l_all, narrow_tiles, dm)
    down_l = load_tiles(l_all, 2 * narrow_tiles, ff)
    gate_r = load_tiles(r_all, 0, ff)
    up_r = load_tiles(r_all, wide_tiles, ff)
    down_r = load_tiles(r_all, 2 * wide_tiles, dm)
    return (grad_input, gate_l, gate_r, up_l, up_r, down_l, down_r)


def solution(mesh):
    fine = Mesh(mesh.devices.reshape(NY, NX, NZ, NC), ("y", "x", "z", "core"))
    both, left, right = P(ROW, COL), P(None, ROW), P(None, COL)
    return jax.shard_map(
        per_device,
        mesh=fine,
        in_specs=(P(COL, ROW), both, both, both, both, left, right, left, right, left, right),
        out_specs=(P(COL, ROW), left, right, left, right, left, right),
        check_vma=False,
    )
```
